32 devices in a mesh: node: 8 (over y, x, core), tm: 4 (over z).
Axes of the slice: x: 2, y: 2, z: 4, core: 2. Of those that a mesh axis runs over, the one named last changes fastest.
Arguments:
- observed: bfloat16 [32768, 4096], P('node', 'tm'), may hold values from 0.5 to 32
- node_factor: bfloat16 [64, 32768], P(None, ('node', 'tm')), may hold values from 0.19921875 to 1
- time_factor: bfloat16 [64, 256], P(None, 'tm'), may hold values from 0.19921875 to 1
- species_factor: bfloat16 [64, 16], replicated, may hold values from 0.19921875 to 1
Outputs:
- grad_node: float32 [64, 32768], P(None, ('node', 'tm'))
- grad_time: float32 [64, 256], P(None, 'tm')
- grad_species: float32 [64, 16], replicated
The draws below stay inside these ranges and needn't reach their ends.
All inputs are finite; a program needn't handle non-finite values.
Results may differ from the reference program's by a relative error of at most 0.0017.
Values may be sent and summed in bfloat16 or wider, within the bound.
A program may use at most 64 MiB of HBM per device.

```python
import math
import jax
import jax.numpy as jnp
from jax import lax

R = 64
S = 16
NODES = 32768
STEPS = 256


def level_of(key, shape, pieces, low, high):
    def one(axis_at, shards_of):
        steps = jax.random.uniform(jax.random.fold_in(jax.random.fold_in(key, 6), axis_at), (shards_of,), jnp.float32, low / len(pieces), high / len(pieces))
        return jnp.repeat(jnp.exp(steps), shape[axis_at] // shards_of).reshape((-1,) + (1,) * (len(shape) - axis_at - 1))

    level = one(*pieces[0])
    for cut in pieces[1:]:
        level = level * one(*cut)
    return level


def setup_inputs(seed: int = 0) -> dict:
    streams_of = jax.random.split(jax.random.key(seed), 5)
    observed = jnp.clip(jnp.exp(math.log(32.0) - 4.158883 * jax.random.uniform(streams_of[0], (NODES, STEPS * S), jnp.float32) ** level_of(streams_of[0], (NODES, STEPS * S), ((0, 8), (1, 4)), -0.2, 0.2)), 0.5, 32.0).astype(jnp.bfloat16)
    node_factor = jnp.clip(jnp.exp(math.log(1.0) - 1.6133518 * jax.random.uniform(streams_of[1], (R, NODES), jnp.float32) ** level_of(streams_of[1], (R, NODES), ((1, 32),), -0.2, 0.2)), 0.19921875, 1.0).astype(jnp.bfloat16)
    time_factor = jnp.clip(jnp.exp(math.log(1.0) - 1.6133518 * jax.random.uniform(streams_of[2], (R, STEPS), jnp.float32) ** level_of(streams_of[2], (R, STEPS), ((1, 4),), -0.2, 0.2)), 0.19921875, 1.0).astype(jnp.bfloat16)
    species_factor = jnp.clip(jnp.exp(jax.random.uniform(streams_of[3], (R, S), jnp.float32, math.log(0.19921875), math.log(1.0))), 0.19921875, 1.0).astype(jnp.bfloat16)
    return dict(observed=observed, node_factor=node_factor, time_factor=time_factor, species_factor=species_factor)


def widen(values):
    return lax.optimization_barrier(values).astype(jnp.float32)

def reference(observed, node_factor, time_factor, species_factor):
    factor_rank = node_factor.shape[0]
    time_vals = time_factor.astype(jnp.float32)
    species_vals = species_factor.astype(jnp.float32)
    khatri = (time_vals[:, :, None] * species_vals[:, None, :]).reshape(factor_rank, STEPS * S).astype(jnp.bfloat16)
    khatri_wide = widen(khatri)
    block_rows = math.gcd(NODES, 4096)
    nblocks = NODES // block_rows
    observed_blocks = observed.reshape(nblocks, block_rows, STEPS * S)
    factor_blocks = node_factor.T.reshape(nblocks, block_rows, factor_rank)

    def absorb_block(contracted, block_pair):
        observed_rows, factor_block = block_pair
        factor_wide = factor_block.astype(jnp.float32)
        modelled = jnp.dot(factor_wide, khatri_wide, precision=lax.Precision.HIGHEST)
        derivative = ((modelled - observed_rows.astype(jnp.float32)) / (modelled * modelled)).astype(jnp.bfloat16)
        derivative_wide = widen(derivative)
        node_part = jnp.dot(derivative_wide, khatri_wide.T, precision=lax.Precision.HIGHEST)
        contracted = contracted + jnp.dot(derivative_wide.T, factor_wide, precision=lax.Precision.HIGHEST)
        return (contracted, node_part)
    start_sum = jnp.zeros((STEPS * S, factor_rank), jnp.float32)
    contracted, node_parts = lax.scan(absorb_block, start_sum, (observed_blocks, factor_blocks))
    grad_node = node_parts.reshape(NODES, factor_rank).T / math.sqrt(STEPS * S)
    by_step = contracted.reshape(STEPS, S, factor_rank)
    grad_time = jnp.einsum('tsr,rs->rt', by_step, species_vals, precision=lax.Precision.HIGHEST) / math.sqrt(NODES * S)
    grad_species = jnp.einsum('tsr,rt->rs', by_step, time_vals, precision=lax.Precision.HIGHEST) / math.sqrt(NODES * STEPS)
    return (grad_node, grad_time, grad_species)
```

```python
import functools
import math

import jax
import jax.numpy as jnp
from jax import lax
from jax.experimental import pallas as pl
from jax.experimental.pallas import tpu as pltpu
from jax.sharding import PartitionSpec as P

MESH = pl.DeviceIdType.MESH
F32 = jnp.float32
BF16 = jnp.bfloat16
LINK = jnp.float32
LOOK = 2
COLS = 256


def kernel(
    nodes_n, tm_n, width, scales,
    obs_ref, nf_ref, tf_ref, sf_ref,
    gnode_ref, gtime_ref, gspec_ref,
    obs_v, gath, mine, out, above, below, khatri, spread_t, spread_s, ctot,
    small, small_in, spec_out, spec_in,
    obs_sem, g_send, g_recv, r_send, a_recv, b_recv, s_send, s_recv, p_send, p_recv,
):
    rank, own = nf_ref.shape
    rows, flat = obs_ref.shape
    steps = tf_ref.shape[1]
    species = sf_ref.shape[1]
    per = own // width
    total = tm_n * per
    lanes = small.shape[1]
    z = lax.axis_index("tm")
    me = lax.axis_index("node")
    top = tm_n - 1
    scale_node, scale_time, scale_spec = scales

    def place(p):
        low = jnp.minimum(z, top - z)
        q = p - per
        k = q // (2 * per) + 1
        w = q % (2 * per)
        pair_owner = jnp.where(w % 2 == 0, z - k, z + k)
        q2 = q - 2 * low * per
        dist = low + 1 + q2 // per
        far_owner = jnp.where(z < top - z, z + dist, z - dist)
        paired = q2 < 0
        owner = jnp.where(p < per, z, jnp.where(paired, pair_owner, far_owner))
        chunk = jnp.where(p < per, p, jnp.where(paired, w // 2, q2 % per))
        return owner, owner * per + chunk

    def obs_copy(g):
        at = pl.ds(pl.multiple_of(g * width, width), width)
        return pltpu.make_async_copy(obs_ref.at[at, :], obs_v.at[at, :], obs_sem.at[g])

    def start_obs(p, _):
        obs_copy(place(p)[1]).start()
        return 0

    def gather_copy(g, up):
        return pltpu.make_async_remote_copy(
            src_ref=gath.at[g], dst_ref=gath.at[g],
            send_sem=g_send.at[1 if up else 0, g], recv_sem=g_recv.at[g],
            device_id={"tm": z + 1 if up else z - 1}, device_id_type=MESH,
        )

    def sum_copy(g, up):
        return pltpu.make_async_remote_copy(
            src_ref=out.at[g], dst_ref=(below if up else above).at[g],
            send_sem=r_send.at[g], recv_sem=(b_recv if up else a_recv).at[g],
            device_id={"tm": z + 1 if up else z - 1}, device_id_type=MESH,
        )

    def small_copy(k):
        return pltpu.make_async_remote_copy(
            src_ref=small, dst_ref=small_in.at[k - 1],
            send_sem=s_send.at[k - 1], recv_sem=s_recv.at[k - 1],
            device_id={"node": lax.rem(me + k, nodes_n)}, device_id_type=MESH,
        )

    def spec_copy(k):
        return pltpu.make_async_remote_copy(
            src_ref=spec_out, dst_ref=spec_in.at[k - 1],
            send_sem=p_send.at[k - 1], recv_sem=p_recv.at[k - 1],
            device_id={"tm": lax.rem(z + k, tm_n)}, device_id_type=MESH,
        )

    barrier = pltpu.get_barrier_semaphore()
    for k in range(1, nodes_n):
        pl.semaphore_signal(
            barrier, inc=1, device_id={"node": lax.rem(me + k, nodes_n)}, device_id_type=MESH
        )
    for k in range(1, tm_n):
        pl.semaphore_signal(
            barrier, inc=1, device_id={"tm": lax.rem(z + k, tm_n)}, device_id_type=MESH
        )
    lax.fori_loop(0, total, start_obs, 0)
    for c in range(per):
        gath[z * per + c] = nf_ref[:, c * width:(c + 1) * width]
    pl.semaphore_wait(barrier, nodes_n - 1 + tm_n - 1)

    def start_gather(c, _):
        g = z * per + c

        @pl.when(z < top)
        def _():
            gather_copy(g, True).start()

        @pl.when(z > 0)
        def _():
            gather_copy(g, False).start()

        return 0

    lax.fori_loop(0, per, start_gather, 0)

    col = lax.broadcasted_iota(jnp.int32, (steps, flat), 1)
    row = lax.broadcasted_iota(jnp.int32, (steps, flat), 0) * species
    wide_t = jnp.where((col >= row) & (col < row + species), 1.0, 0.0).astype(BF16)
    col_s = lax.rem(lax.broadcasted_iota(jnp.int32, (species, flat), 1), species)
    row_s = lax.broadcasted_iota(jnp.int32, (species, flat), 0)
    wide_s = jnp.where(col_s == row_s, 1.0, 0.0).astype(BF16)
    spread_t[...] = jnp.dot(tf_ref[...], wide_t, preferred_element_type=F32)
    spread_s[...] = jnp.dot(sf_ref[...], wide_s, preferred_element_type=F32)
    khatri[...] = (spread_t[...] * spread_s[...]).astype(BF16)
    ctot[...] = jnp.zeros_like(ctot)

    def relay(p):
        owner, g = place(p)

        @pl.when(owner != z)
        def _():
            gather_copy(g, True).wait_recv()

        @pl.when((owner < z) & (z < top))
        def _():
            gather_copy(g, True).start()

        @pl.when((owner > z) & (z > 0))
        def _():
            gather_copy(g, False).start()

    def compute(g):
        obs_copy(g).wait()
        factor = gath[g]
        at = pl.ds(pl.multiple_of(g * width, width), width)
        part = jnp.zeros((rank, width), F32)
        for c in range(0, flat, COLS):
            kh = khatri[:, c:c + COLS]
            modelled = lax.dot_general(
                factor, kh, (((0,), (0,)), ((), ())), preferred_element_type=F32
            )
            gap = modelled - obs_v[at, c:c + COLS].astype(F32)
            derivative = (gap / (modelled * modelled)).astype(BF16)
            part = part + lax.dot_general(
                kh, derivative, (((1,), (1,)), ((), ())), preferred_element_type=F32
            )
            ctot[:, c:c + COLS] += jnp.dot(factor, derivative, preferred_element_type=F32)
        return part

    def step(p, _):
        @pl.when(p + LOOK < total)
        def _():
            relay(p + LOOK)

        owner, g = place(p)
        part = compute(g)
        mine[g] = part

        @pl.when((z == top) & (owner < z))
        def _():
            out[g] = part.astype(out.dtype)
            sum_copy(g, False).start()

        @pl.when((z == 0) & (owner > z))
        def _():
            out[g] = part.astype(out.dtype)
            sum_copy(g, True).start()

        return 0

    for p in range(LOOK):
        relay(p)
    lax.fori_loop(0, total, step, 0)

    time_col = lax.broadcasted_iota(jnp.int32, (flat, lanes), 1)
    time_row = lax.broadcasted_iota(jnp.int32, (flat, lanes), 0)
    at_step = time_col * species
    pick_t = jnp.where((time_row >= at_step) & (time_row < at_step + species), 1.0, 0.0)
    pick_s = jnp.where(lax.rem(time_row, species) == time_col - steps, 1.0, 0.0)
    small[...] = jnp.dot(
        ctot[...] * spread_s[...], pick_t, precision=lax.Precision.HIGHEST,
        preferred_element_type=F32,
    ) + jnp.dot(
        ctot[...] * spread_t[...], pick_s, precision=lax.Precision.HIGHEST,
        preferred_element_type=F32,
    )
    for k in range(1, nodes_n):
        small_copy(k).start()

    def pass_up(g, _):
        sum_copy(g, True).wait_recv()
        out[g] = (mine[g] + below[g].astype(F32)).astype(out.dtype)
        sum_copy(g, True).start()
        return 0

    def pass_down(g, _):
        sum_copy(g, False).wait_recv()
        out[g] = (mine[g] + above[g].astype(F32)).astype(out.dtype)
        sum_copy(g, False).start()
        return 0

    def all_down():
        def owner_down(i, _):
            first = (z - 1 - i) * per
            return lax.fori_loop(first, first + per, pass_down, 0)

        lax.fori_loop(0, z, owner_down, 0)

    def all_up():
        lax.fori_loop((z + 1) * per, total, pass_up, 0)

    inner = (z > 0) & (z < top)

    @pl.when(inner & (2 * z < top))
    def _():
        all_up()
        all_down()

    @pl.when(inner & (2 * z >= top))
    def _():
        all_down()
        all_up()

    summed = small[...]
    for k in range(1, nodes_n):
        small_copy(k).wait_recv()
        summed = summed + small_in[k - 1]
    spec_out[...] = summed
    for k in range(1, tm_n):
        spec_copy(k).start()
    gtime_ref[...] = summed[:, :steps] * scale_time

    def finish(c, _):
        g = z * per + c

        @pl.when(z < top)
        def _():
            sum_copy(g, False).wait_recv()
            mine[g] += above[g].astype(F32)

        @pl.when(z > 0)
        def _():
            sum_copy(g, True).wait_recv()
            mine[g] += below[g].astype(F32)

        return 0

    lax.fori_loop(0, per, finish, 0)
    for c in range(per):
        gnode_ref[:, c * width:(c + 1) * width] = mine[z * per + c] * scale_node

    for k in range(1, tm_n):
        spec_copy(k).wait_recv()
        summed = summed + spec_in[k - 1]
    gspec_ref[...] = summed[:, steps:steps + species] * scale_spec

    def drain(p, _):
        owner, g = place(p)

        @pl.when((owner <= z) & (z < top))
        def _():
            gather_copy(g, True).wait_send()

        @pl.when((owner >= z) & (z > 0))
        def _():
            gather_copy(g, False).wait_send()

        @pl.when(owner > z)
        def _():
            sum_copy(g, True).wait_send()

        @pl.when(owner < z)
        def _():
            sum_copy(g, False).wait_send()

        return 0

    lax.fori_loop(0, total, drain, 0)
    for k in range(1, nodes_n):
        small_copy(k).wait_send()
    for k in range(1, tm_n):
        spec_copy(k).wait_send()


def shards(nodes_n, tm_n, observed, node_factor, time_factor, species_factor):
    rank, own = node_factor.shape
    rows, flat = observed.shape
    steps, species = time_factor.shape[1], species_factor.shape[1]
    width = min(own, 256)
    total = rows // width
    lanes = 128 * ((steps + species + 127) // 128)
    nodes_all, steps_all = rows * nodes_n, steps * tm_n
    scales = (
        1.0 / math.sqrt(steps_all * species),
        1.0 / math.sqrt(nodes_all * species),
        1.0 / math.sqrt(nodes_all * steps_all),
    )
    vmem = pl.BlockSpec(memory_space=pltpu.VMEM)
    dma = pltpu.SemaphoreType.DMA
    return pl.pallas_call(
        functools.partial(kernel, nodes_n, tm_n, width, scales),
        out_shape=(
            jax.ShapeDtypeStruct((rank, own), F32),
            jax.ShapeDtypeStruct((rank, steps), F32),
            jax.ShapeDtypeStruct((rank, species), F32),
        ),
        in_specs=[pl.BlockSpec(memory_space=pl.ANY), vmem, vmem, vmem],
        out_specs=(vmem, vmem, vmem),
        scratch_shapes=[
            pltpu.VMEM((rows, flat), BF16),
            pltpu.VMEM((total, rank, width), BF16),
            pltpu.VMEM((total, rank, width), F32),
            pltpu.VMEM((total, rank, width), LINK),
            pltpu.VMEM((total, rank, width), LINK),
            pltpu.VMEM((total, rank, width), LINK),
            pltpu.VMEM((rank, flat), BF16),
            pltpu.VMEM((rank, flat), F32),
            pltpu.VMEM((rank, flat), F32),
            pltpu.VMEM((rank, flat), F32),
            pltpu.VMEM((rank, lanes), F32),
            pltpu.VMEM((nodes_n - 1, rank, lanes), F32),
            pltpu.VMEM((rank, lanes), F32),
            pltpu.VMEM((tm_n - 1, rank, lanes), F32),
            dma((total,)),
            dma((2, total)),
            dma((total,)),
            dma((total,)),
            dma((total,)),
            dma((total,)),
            dma((nodes_n - 1,)),
            dma((nodes_n - 1,)),
            dma((tm_n - 1,)),
            dma((tm_n - 1,)),
        ],
        compiler_params=pltpu.CompilerParams(
            collective_id=0, has_side_effects=True, vmem_limit_bytes=48 * 1024 * 1024
        ),
        cost_estimate=pl.CostEstimate(
            flops=6 * rows * flat * rank, bytes_accessed=2 * rows * flat, transcendentals=0
        ),
    )(observed, node_factor, time_factor, species_factor)


def solution(mesh):
    in_specs = (P("node", "tm"), P(None, ("node", "tm")), P(None, "tm"), P())
    out_specs = (P(None, ("node", "tm")), P(None, "tm"), P())
    body = functools.partial(shards, mesh.shape["node"], mesh.shape["tm"])
    return jax.shard_map(body, mesh=mesh, in_specs=in_specs, out_specs=out_specs, check_vma=False)
```

```python
import functools
import math

import jax
import jax.numpy as jnp
from jax import lax
from jax.experimental import pallas as pl
from jax.experimental.pallas import tpu as pltpu
from jax.sharding import PartitionSpec as P

MESH = pl.DeviceIdType.MESH
F32 = jnp.float32
BF16 = jnp.bfloat16
LOOK = 2
COLS = 1024


def kernel(
    nodes_n, tm_n, width, scales,
    obs_ref, nf_ref, tf_ref, sf_ref,
    gnode_ref, gtime_ref, gspec_ref,
    obs_v, gath, mine, out, above, below, out_w, above_w, below_w, khatri, spread_t, spread_s, ctot,
    small, small_in, spec_out, spec_in,
    obs_sem, g_send, g_recv, r_send, a_recv, b_recv, s_send, s_recv, p_send, p_recv,
):
    rank, own = nf_ref.shape
    rows, flat = obs_ref.shape
    steps = tf_ref.shape[1]
    species = sf_ref.shape[1]
    per = own // width
    total = tm_n * per
    lanes = small.shape[1]
    z = lax.axis_index("tm")
    me = lax.axis_index("node")
    top = tm_n - 1
    scale_node, scale_time, scale_spec = scales

    def place(p):
        low = jnp.minimum(z, top - z)
        q = p - per
        k = q // (2 * per) + 1
        w = q % (2 * per)
        pair_owner = jnp.where(w % 2 == 0, z - k, z + k)
        q2 = q - 2 * low * per
        dist = low + 1 + q2 // per
        far_owner = jnp.where(z < top - z, z + dist, z - dist)
        paired = q2 < 0
        owner = jnp.where(p < per, z, jnp.where(paired, pair_owner, far_owner))
        chunk = jnp.where(p < per, p, jnp.where(paired, w // 2, q2 % per))
        return owner, owner * per + chunk

    def obs_copy(g):
        at = pl.ds(pl.multiple_of(g * width, width), width)
        return pltpu.make_async_copy(obs_ref.at[at, :], obs_v.at[at, :], obs_sem.at[g])

    def start_obs(p, _):
        obs_copy(place(p)[1]).start()
        return 0

    def gather_copy(g, up):
        return pltpu.make_async_remote_copy(
            src_ref=gath.at[g], dst_ref=gath.at[g],
            send_sem=g_send.at[1 if up else 0, g], recv_sem=g_recv.at[g],
            device_id={"tm": z + 1 if up else z - 1}, device_id_type=MESH,
        )

    def sum_copy(g, up, wide):
        source = out_w if wide else out
        target = (below_w if up else above_w) if wide else (below if up else above)
        return pltpu.make_async_remote_copy(
            src_ref=source.at[g], dst_ref=target.at[g],
            send_sem=r_send.at[g], recv_sem=(b_recv if up else a_recv).at[g],
            device_id={"tm": z + 1 if up else z - 1}, device_id_type=MESH,
        )

    def by_type(terms, act):
        if tm_n <= 3:
            act(False)
            return

        @pl.when(terms >= 3)
        def _():
            act(True)

        @pl.when(terms < 3)
        def _():
            act(False)

    def send_sum(g, up, value):
        def act(wide):
            if wide:
                out_w[g] = value
            else:
                out[g] = value.astype(BF16)
            sum_copy(g, up, wide).start()

        by_type(z + 1 if up else tm_n - z, act)

    def take_sum(g, up):
        def act(wide):
            sum_copy(g, up, wide).wait_recv()
            if wide:
                mine[g] += (below_w if up else above_w)[g]
            else:
                mine[g] += (below if up else above)[g].astype(F32)

        by_type(z if up else top - z, act)

    def sent_sum(g, up):
        by_type(z + 1 if up else tm_n - z, lambda wide: sum_copy(g, up, wide).wait_send())

    def small_copy(k):
        return pltpu.make_async_remote_copy(
            src_ref=small, dst_ref=small_in.at[k - 1],
            send_sem=s_send.at[k - 1], recv_sem=s_recv.at[k - 1],
            device_id={"node": lax.rem(me + k, nodes_n)}, device_id_type=MESH,
        )

    def spec_copy(k):
        return pltpu.make_async_remote_copy(
            src_ref=spec_out, dst_ref=spec_in.at[k - 1],
            send_sem=p_send.at[k - 1], recv_sem=p_recv.at[k - 1],
            device_id={"tm": lax.rem(z + k, tm_n)}, device_id_type=MESH,
        )

    barrier = pltpu.get_barrier_semaphore()
    for k in range(1, nodes_n):
        pl.semaphore_signal(
            barrier, inc=1, device_id={"node": lax.rem(me + k, nodes_n)}, device_id_type=MESH
        )
    for k in range(1, tm_n):
        pl.semaphore_signal(
            barrier, inc=1, device_id={"tm": lax.rem(z + k, tm_n)}, device_id_type=MESH
        )
    lax.fori_loop(0, total, start_obs, 0)
    for c in range(per):
        gath[z * per + c] = nf_ref[:, c * width:(c + 1) * width]
    pl.semaphore_wait(barrier, nodes_n - 1 + tm_n - 1)

    def start_gather(c, _):
        g = z * per + c

        @pl.when(z < top)
        def _():
            gather_copy(g, True).start()

        @pl.when(z > 0)
        def _():
            gather_copy(g, False).start()

        return 0

    lax.fori_loop(0, per, start_gather, 0)

    col = lax.broadcasted_iota(jnp.int32, (steps, flat), 1)
    row = lax.broadcasted_iota(jnp.int32, (steps, flat), 0) * species
    wide_t = jnp.where((col >= row) & (col < row + species), 1.0, 0.0).astype(BF16)
    col_s = lax.rem(lax.broadcasted_iota(jnp.int32, (species, flat), 1), species)
    row_s = lax.broadcasted_iota(jnp.int32, (species, flat), 0)
    wide_s = jnp.where(col_s == row_s, 1.0, 0.0).astype(BF16)
    spread_t[...] = jnp.dot(tf_ref[...], wide_t, preferred_element_type=F32)
    spread_s[...] = jnp.dot(sf_ref[...], wide_s, preferred_element_type=F32)
    khatri[...] = (spread_t[...] * spread_s[...]).astype(BF16)
    ctot[...] = jnp.zeros_like(ctot)

    def relay(p):
        owner, g = place(p)

        @pl.when(owner != z)
        def _():
            gather_copy(g, True).wait_recv()

        @pl.when((owner < z) & (z < top))
        def _():
            gather_copy(g, True).start()

        @pl.when((owner > z) & (z > 0))
        def _():
            gather_copy(g, False).start()

    def compute(g):
        obs_copy(g).wait()
        factor = gath[g]
        at = pl.ds(pl.multiple_of(g * width, width), width)
        part = jnp.zeros((rank, width), F32)
        for c in range(0, flat, COLS):
            kh = khatri[:, c:c + COLS]
            modelled = lax.dot_general(
                factor, kh, (((0,), (0,)), ((), ())), preferred_element_type=F32
            )
            gap = modelled - obs_v[at, c:c + COLS].astype(F32)
            derivative = (gap / (modelled * modelled)).astype(BF16)
            part = part + lax.dot_general(
                kh, derivative, (((1,), (1,)), ((), ())), preferred_element_type=F32
            )
            ctot[:, c:c + COLS] += jnp.dot(factor, derivative, preferred_element_type=F32)
        return part

    def step(p, _):
        @pl.when(p + LOOK < total)
        def _():
            relay(p + LOOK)

        owner, g = place(p)
        part = compute(g)
        mine[g] = part

        @pl.when((z == top) & (owner < z))
        def _():
            send_sum(g, False, part)

        @pl.when((z == 0) & (owner > z))
        def _():
            send_sum(g, True, part)

        return 0

    for p in range(LOOK):
        relay(p)
    lax.fori_loop(0, total, step, 0)

    time_col = lax.broadcasted_iota(jnp.int32, (flat, lanes), 1)
    time_row = lax.broadcasted_iota(jnp.int32, (flat, lanes), 0)
    at_step = time_col * species
    pick_t = jnp.where((time_row >= at_step) & (time_row < at_step + species), 1.0, 0.0)
    pick_s = jnp.where(lax.rem(time_row, species) == time_col - steps, 1.0, 0.0)
    small[...] = jnp.dot(
        ctot[...] * spread_s[...], pick_t, precision=lax.Precision.HIGHEST,
        preferred_element_type=F32,
    ) + jnp.dot(
        ctot[...] * spread_t[...], pick_s, precision=lax.Precision.HIGHEST,
        preferred_element_type=F32,
    )
    for k in range(1, nodes_n):
        small_copy(k).start()

    def pass_up(g, _):
        take_sum(g, True)
        send_sum(g, True, mine[g])
        return 0

    def pass_down(g, _):
        take_sum(g, False)
        send_sum(g, False, mine[g])
        return 0

    def all_down():
        def owner_down(i, _):
            first = (z - 1 - i) * per
            return lax.fori_loop(first, first + per, pass_down, 0)

        lax.fori_loop(0, z, owner_down, 0)

    def all_up():
        lax.fori_loop((z + 1) * per, total, pass_up, 0)

    inner = (z > 0) & (z < top)

    @pl.when(inner & (2 * z < top))
    def _():
        all_up()
        all_down()

    @pl.when(inner & (2 * z >= top))
    def _():
        all_down()
        all_up()

    summed = small[...]
    for k in range(1, nodes_n):
        small_copy(k).wait_recv()
        summed = summed + small_in[k - 1]
    spec_out[...] = summed
    for k in range(1, tm_n):
        spec_copy(k).start()
    gtime_ref[...] = summed[:, :steps] * scale_time

    def finish(c, _):
        g = z * per + c

        @pl.when(z < top)
        def _():
            take_sum(g, False)

        @pl.when(z > 0)
        def _():
            take_sum(g, True)

        return 0

    lax.fori_loop(0, per, finish, 0)
    for c in range(per):
        gnode_ref[:, c * width:(c + 1) * width] = mine[z * per + c] * scale_node

    for k in range(1, tm_n):
        spec_copy(k).wait_recv()
        summed = summed + spec_in[k - 1]
    gspec_ref[...] = summed[:, steps:steps + species] * scale_spec

    def drain(p, _):
        owner, g = place(p)

        @pl.when((owner <= z) & (z < top))
        def _():
            gather_copy(g, True).wait_send()

        @pl.when((owner >= z) & (z > 0))
        def _():
            gather_copy(g, False).wait_send()

        @pl.when(owner > z)
        def _():
            sent_sum(g, True)

        @pl.when(owner < z)
        def _():
            sent_sum(g, False)

        return 0

    lax.fori_loop(0, total, drain, 0)
    for k in range(1, nodes_n):
        small_copy(k).wait_send()
    for k in range(1, tm_n):
        spec_copy(k).wait_send()


def shards(nodes_n, tm_n, observed, node_factor, time_factor, species_factor):
    rank, own = node_factor.shape
    rows, flat = observed.shape
    steps, species = time_factor.shape[1], species_factor.shape[1]
    width = min(own, 256)
    total = rows // width
    lanes = 128 * ((steps + species + 127) // 128)
    nodes_all, steps_all = rows * nodes_n, steps * tm_n
    scales = (
        1.0 / math.sqrt(steps_all * species),
        1.0 / math.sqrt(nodes_all * species),
        1.0 / math.sqrt(nodes_all * steps_all),
    )
    vmem = pl.BlockSpec(memory_space=pltpu.VMEM)
    dma = pltpu.SemaphoreType.DMA
    return pl.pallas_call(
        functools.partial(kernel, nodes_n, tm_n, width, scales),
        out_shape=(
            jax.ShapeDtypeStruct((rank, own), F32),
            jax.ShapeDtypeStruct((rank, steps), F32),
            jax.ShapeDtypeStruct((rank, species), F32),
        ),
        in_specs=[pl.BlockSpec(memory_space=pl.ANY), vmem, vmem, vmem],
        out_specs=(vmem, vmem, vmem),
        scratch_shapes=[
            pltpu.VMEM((rows, flat), BF16),
            pltpu.VMEM((total, rank, width), BF16),
            pltpu.VMEM((total, rank, width), F32),
            pltpu.VMEM((total, rank, width), BF16),
            pltpu.VMEM((total, rank, width), BF16),
            pltpu.VMEM((total, rank, width), BF16),
            pltpu.VMEM((total, rank, width), F32),
            pltpu.VMEM((total, rank, width), F32),
            pltpu.VMEM((total, rank, width), F32),
            pltpu.VMEM((rank, flat), BF16),
            pltpu.VMEM((rank, flat), F32),
            pltpu.VMEM((rank, flat), F32),
            pltpu.VMEM((rank, flat), F32),
            pltpu.VMEM((rank, lanes), F32),
            pltpu.VMEM((nodes_n - 1, rank, lanes), F32),
            pltpu.VMEM((rank, lanes), F32),
            pltpu.VMEM((tm_n - 1, rank, lanes), F32),
            dma((total,)),
            dma((2, total)),
            dma((total,)),
            dma((total,)),
            dma((total,)),
            dma((total,)),
            dma((nodes_n - 1,)),
            dma((nodes_n - 1,)),
            dma((tm_n - 1,)),
            dma((tm_n - 1,)),
        ],
        compiler_params=pltpu.CompilerParams(
            collective_id=0, has_side_effects=True, vmem_limit_bytes=48 * 1024 * 1024
        ),
        cost_estimate=pl.CostEstimate(
            flops=6 * rows * flat * rank, bytes_accessed=2 * rows * flat, transcendentals=0
        ),
    )(observed, node_factor, time_factor, species_factor)


def solution(mesh):
    in_specs = (P("node", "tm"), P(None, ("node", "tm")), P(None, "tm"), P())
    out_specs = (P(None, ("node", "tm")), P(None, "tm"), P())
    body = functools.partial(shards, mesh.shape["node"], mesh.shape["tm"])
    return jax.shard_map(body, mesh=mesh, in_specs=in_specs, out_specs=out_specs, check_vma=False)
```

```python
import functools
import math

import jax
import jax.numpy as jnp
from jax import lax
from jax.experimental import pallas as pl
from jax.experimental.pallas import tpu as pltpu
from jax.sharding import PartitionSpec as P

MESH = pl.DeviceIdType.MESH
F32 = jnp.float32
BF16 = jnp.bfloat16
LOOK = 2
COLS = 1024


def kernel(
    nodes_n, tm_n, width, scales,
    obs_ref, nf_ref, tf_hbm, sf_hbm,
    gnode_ref, gtime_ref, gspec_ref,
    obs_v, gath, mine, out, above, below, out_w, above_w, below_w, khatri, spread_t, spread_s, ctot, wide, tf_ref, sf_ref,
    small, small_in, spec_out, spec_in,
    obs_sem, g_send, g_recv, r_send, a_recv, b_recv, s_send, s_recv, p_send, p_recv, nf_sem, f_sem,
):
    rank, own = nf_ref.shape
    rows, flat = obs_ref.shape
    steps = tf_ref.shape[1]
    species = sf_ref.shape[0]
    per = own // width
    total = tm_n * per
    z = lax.axis_index("tm")
    me = lax.axis_index("node")
    top = tm_n - 1
    inner = (z > 0) & (z < top)
    low_half = 2 * z < top
    early = tm_n <= 4
    scale_node, scale_time, scale_spec = scales

    def place(p):
        low = jnp.minimum(z, top - z)
        q = p - per
        k = q // (2 * per) + 1
        w = q % (2 * per)
        pair_owner = jnp.where(w % 2 == 0, z - k, z + k)
        q2 = q - 2 * low * per
        dist = low + 1 + q2 // per
        far_owner = jnp.where(z < top - z, z + dist, z - dist)
        paired = q2 < 0
        owner = jnp.where(p < per, z, jnp.where(paired, pair_owner, far_owner))
        chunk = jnp.where(p < per, p, jnp.where(paired, w // 2, q2 % per))
        return owner, owner * per + chunk

    def obs_copy(g):
        at = pl.ds(pl.multiple_of(g * width, width), width)
        return pltpu.make_async_copy(obs_ref.at[at, :], obs_v.at[at, :], obs_sem.at[g])

    def start_obs(p, _):
        obs_copy(place(p)[1]).start()
        return 0

    def gather_copy(g, up):
        return pltpu.make_async_remote_copy(
            src_ref=gath.at[g], dst_ref=gath.at[g],
            send_sem=g_send.at[1 if up else 0, g], recv_sem=g_recv.at[g],
            device_id={"tm": z + 1 if up else z - 1}, device_id_type=MESH,
        )

    def sum_copy(g, up, wide):
        source = out_w if wide else out
        target = (below_w if up else above_w) if wide else (below if up else above)
        return pltpu.make_async_remote_copy(
            src_ref=source.at[g], dst_ref=target.at[g],
            send_sem=r_send.at[g], recv_sem=(b_recv if up else a_recv).at[g],
            device_id={"tm": z + 1 if up else z - 1}, device_id_type=MESH,
        )

    def by_type(terms, act):
        if tm_n <= 3:
            act(False)
            return

        @pl.when(terms >= 3)
        def _():
            act(True)

        @pl.when(terms < 3)
        def _():
            act(False)

    def send_sum(g, up, value):
        def act(wide):
            if wide:
                out_w[g] = value
            else:
                out[g] = value.astype(BF16)
            sum_copy(g, up, wide).start()

        by_type(z + 1 if up else tm_n - z, act)

    def take_sum(g, up):
        def act(wide):
            sum_copy(g, up, wide).wait_recv()
            if wide:
                mine[g] += (below_w if up else above_w)[g]
            else:
                mine[g] += (below if up else above)[g].astype(F32)

        by_type(z if up else top - z, act)

    def sent_sum(g, up):
        by_type(z + 1 if up else tm_n - z, lambda wide: sum_copy(g, up, wide).wait_send())

    def small_copy(k):
        return pltpu.make_async_remote_copy(
            src_ref=small, dst_ref=small_in.at[k - 1],
            send_sem=s_send.at[k - 1], recv_sem=s_recv.at[k - 1],
            device_id={"node": lax.rem(me + k, nodes_n)}, device_id_type=MESH,
        )

    def spec_copy(k):
        return pltpu.make_async_remote_copy(
            src_ref=spec_out, dst_ref=spec_in.at[k - 1],
            send_sem=p_send.at[k - 1], recv_sem=p_recv.at[k - 1],
            device_id={"tm": lax.rem(z + k, tm_n)}, device_id_type=MESH,
        )

    barrier = pltpu.get_barrier_semaphore()
    for k in range(1, nodes_n):
        pl.semaphore_signal(
            barrier, inc=1, device_id={"node": lax.rem(me + k, nodes_n)}, device_id_type=MESH
        )
    for k in range(1, tm_n):
        pl.semaphore_signal(
            barrier, inc=1, device_id={"tm": lax.rem(z + k, tm_n)}, device_id_type=MESH
        )
    time_copy = pltpu.make_async_copy(tf_hbm, tf_ref, f_sem.at[0])
    species_copy = pltpu.make_async_copy(sf_hbm, sf_ref, f_sem.at[1])
    time_copy.start()
    species_copy.start()
    own_copies = [
        pltpu.make_async_copy(
            nf_ref.at[:, c * width:(c + 1) * width], gath.at[z * per + c], nf_sem.at[c]
        )
        for c in range(per)
    ]
    for copy in own_copies:
        copy.start()
    lax.fori_loop(0, total, start_obs, 0)
    col = lax.broadcasted_iota(jnp.int32, (steps, flat), 1)
    row = lax.broadcasted_iota(jnp.int32, (steps, flat), 0) * species
    wide[:steps, :] = jnp.where((col >= row) & (col < row + species), 1.0, 0.0).astype(BF16)
    col_s = lax.rem(lax.broadcasted_iota(jnp.int32, (species, flat), 1), species)
    row_s = lax.broadcasted_iota(jnp.int32, (species, flat), 0)
    wide[steps:, :] = jnp.where(col_s == row_s, 1.0, 0.0).astype(BF16)
    time_copy.wait()
    species_copy.wait()
    spread_t[...] = jnp.dot(tf_ref[...], wide[:steps, :], preferred_element_type=F32)
    spread_s[...] = lax.dot_general(
        sf_ref[...], wide[steps:, :], (((0,), (0,)), ((), ())), preferred_element_type=F32
    )
    khatri[...] = (spread_t[...] * spread_s[...]).astype(BF16)
    ctot[...] = jnp.zeros_like(ctot)
    for copy in own_copies:
        copy.wait()
    pl.semaphore_wait(barrier, nodes_n - 1 + tm_n - 1)

    def start_gather(c, _):
        g = z * per + c

        @pl.when(z < top)
        def _():
            gather_copy(g, True).start()

        @pl.when(z > 0)
        def _():
            gather_copy(g, False).start()

        return 0

    lax.fori_loop(0, per, start_gather, 0)

    def relay(p):
        owner, g = place(p)

        @pl.when(owner != z)
        def _():
            gather_copy(g, True).wait_recv()

        @pl.when((owner < z) & (z < top))
        def _():
            gather_copy(g, True).start()

        @pl.when((owner > z) & (z > 0))
        def _():
            gather_copy(g, False).start()

    def compute(g):
        obs_copy(g).wait()
        factor = gath[g]
        at = pl.ds(pl.multiple_of(g * width, width), width)
        part = jnp.zeros((rank, width), F32)
        for c in range(0, flat, COLS):
            kh = khatri[:, c:c + COLS]
            modelled = lax.dot_general(
                factor, kh, (((0,), (0,)), ((), ())), preferred_element_type=F32
            )
            gap = modelled - obs_v[at, c:c + COLS].astype(F32)
            derivative = (gap / (modelled * modelled)).astype(BF16)
            part = part + lax.dot_general(
                kh, derivative, (((1,), (1,)), ((), ())), preferred_element_type=F32
            )
            ctot[:, c:c + COLS] += jnp.dot(factor, derivative, preferred_element_type=F32)
        return part

    def pass_up(g, _):
        take_sum(g, True)
        send_sum(g, True, mine[g])
        return 0

    def pass_down(g, _):
        take_sum(g, False)
        send_sum(g, False, mine[g])
        return 0

    def step(p, _):
        @pl.when(p + LOOK < total)
        def _():
            relay(p + LOOK)

        owner, g = place(p)
        part = compute(g)
        mine[g] = part

        @pl.when((z == top) & (owner < z))
        def _():
            send_sum(g, False, part)

        @pl.when((z == 0) & (owner > z))
        def _():
            send_sum(g, True, part)

        if early:
            @pl.when((p >= total - per) & inner & low_half)
            def _():
                pass_up((z + 1) * per + p - (total - per), 0)

            @pl.when((p >= total - per) & inner & jnp.logical_not(low_half))
            def _():
                pass_down((z - 1) * per + p - (total - per), 0)

        return 0

    for p in range(LOOK):
        relay(p)
    lax.fori_loop(0, total, step, 0)

    def fold(pick, values):
        result = jnp.zeros((pick.shape[0], rank), F32)
        for _ in range(3):
            term = values.astype(BF16)
            values = values - term.astype(F32)
            result = result + lax.dot_general(
                pick, term, (((1,), (1,)), ((), ())), preferred_element_type=F32
            )
        return result

    small[:steps, :] = fold(wide[:steps, :], ctot[...] * spread_s[...])
    small[steps:, :] = fold(wide[steps:, :], ctot[...] * spread_t[...])
    for k in range(1, nodes_n):
        small_copy(k).start()

    def all_down(skip):
        def owner_down(i, _):
            first = (z - 1 - i) * per
            return lax.fori_loop(first, first + per, pass_down, 0)

        lax.fori_loop(skip, z, owner_down, 0)

    def all_up(skip):
        lax.fori_loop((z + 1 + skip) * per, total, pass_up, 0)

    done = 1 if early else 0

    @pl.when(inner & low_half)
    def _():
        all_up(done)
        all_down(0)

    @pl.when(inner & jnp.logical_not(low_half))
    def _():
        all_down(done)
        all_up(0)

    summed = small[...]
    for k in range(1, nodes_n):
        small_copy(k).wait_recv()
        summed = summed + small_in[k - 1]
    spec_out[...] = summed[steps:, :]
    spec_sum = summed[steps:, :]
    for k in range(1, tm_n):
        spec_copy(k).start()
    gtime_ref[...] = summed[:steps, :].T * scale_time

    def finish(c, _):
        g = z * per + c

        @pl.when(z < top)
        def _():
            take_sum(g, False)

        @pl.when(z > 0)
        def _():
            take_sum(g, True)

        return 0

    lax.fori_loop(0, per, finish, 0)
    for c in range(per):
        gnode_ref[:, c * width:(c + 1) * width] = mine[z * per + c] * scale_node

    for k in range(1, tm_n):
        spec_copy(k).wait_recv()
        spec_sum = spec_sum + spec_in[k - 1]
    gspec_ref[...] = spec_sum * scale_spec

    def drain(p, _):
        owner, g = place(p)

        @pl.when((owner <= z) & (z < top))
        def _():
            gather_copy(g, True).wait_send()

        @pl.when((owner >= z) & (z > 0))
        def _():
            gather_copy(g, False).wait_send()

        @pl.when(owner > z)
        def _():
            sent_sum(g, True)

        @pl.when(owner < z)
        def _():
            sent_sum(g, False)

        return 0

    lax.fori_loop(0, total, drain, 0)
    for k in range(1, nodes_n):
        small_copy(k).wait_send()
    for k in range(1, tm_n):
        spec_copy(k).wait_send()


def shards(nodes_n, tm_n, observed, node_factor, time_factor, species_factor):
    rank, own = node_factor.shape
    rows, flat = observed.shape
    steps, species = time_factor.shape[1], species_factor.shape[1]
    width = min(own, 256)
    total = rows // width
    both = steps + species
    nodes_all, steps_all = rows * nodes_n, steps * tm_n
    scales = (
        1.0 / math.sqrt(steps_all * species),
        1.0 / math.sqrt(nodes_all * species),
        1.0 / math.sqrt(nodes_all * steps_all),
    )
    vmem = pl.BlockSpec(memory_space=pltpu.VMEM)
    dma = pltpu.SemaphoreType.DMA
    anywhere = pl.BlockSpec(memory_space=pl.ANY)
    grad_node, grad_time, grad_species = pl.pallas_call(
        functools.partial(kernel, nodes_n, tm_n, width, scales),
        out_shape=(
            jax.ShapeDtypeStruct((rank, own), F32),
            jax.ShapeDtypeStruct((rank, steps), F32),
            jax.ShapeDtypeStruct((species, rank), F32),
        ),
        in_specs=[anywhere] * 4,
        out_specs=(vmem, vmem, vmem),
        scratch_shapes=[
            pltpu.VMEM((rows, flat), BF16),
            pltpu.VMEM((total, rank, width), BF16),
            pltpu.VMEM((total, rank, width), F32),
            pltpu.VMEM((total, rank, width), BF16),
            pltpu.VMEM((total, rank, width), BF16),
            pltpu.VMEM((total, rank, width), BF16),
            pltpu.VMEM((total, rank, width), F32),
            pltpu.VMEM((total, rank, width), F32),
            pltpu.VMEM((total, rank, width), F32),
            pltpu.VMEM((rank, flat), BF16),
            pltpu.VMEM((rank, flat), F32),
            pltpu.VMEM((rank, flat), F32),
            pltpu.VMEM((rank, flat), F32),
            pltpu.VMEM((both, flat), BF16),
            pltpu.VMEM((rank, steps), BF16),
            pltpu.VMEM((species, rank), BF16),
            pltpu.VMEM((both, rank), F32),
            pltpu.VMEM((nodes_n - 1, both, rank), F32),
            pltpu.VMEM((species, rank), F32),
            pltpu.VMEM((tm_n - 1, species, rank), F32),
            dma((total,)),
            dma((2, total)),
            dma((total,)),
            dma((total,)),
            dma((total,)),
            dma((total,)),
            dma((nodes_n - 1,)),
            dma((nodes_n - 1,)),
            dma((tm_n - 1,)),
            dma((tm_n - 1,)),
            dma((own // width,)),
            dma((2,)),
        ],
        compiler_params=pltpu.CompilerParams(
            collective_id=0, has_side_effects=True, vmem_limit_bytes=56 * 1024 * 1024
        ),
        cost_estimate=pl.CostEstimate(
            flops=6 * rows * flat * rank, bytes_accessed=2 * rows * flat, transcendentals=0
        ),
    )(observed, node_factor, time_factor, species_factor.T)
    return grad_node, grad_time, grad_species.T


def solution(mesh):
    in_specs = (P("node", "tm"), P(None, ("node", "tm")), P(None, "tm"), P())
    out_specs = (P(None, ("node", "tm")), P(None, "tm"), P())
    body = functools.partial(shards, mesh.shape["node"], mesh.shape["tm"])
    return jax.shard_map(body, mesh=mesh, in_specs=in_specs, out_specs=out_specs, check_vma=False)
```
